256 devices in a mesh: dp: 256 (over z, y, x, core).
Axes of the slice: x: 4, y: 4, z: 8, core: 2. Of those that a mesh axis runs over, the one named last changes fastest.
Arguments:
- image_emb: bfloat16 [196608, 1152], P('dp'), may hold values from -0.19921875 to 0.19921875
- text_emb: bfloat16 [196608, 1152], P('dp'), may hold values from -0.19921875 to 0.19921875
- round_masks: int32 [2], replicated, may hold values from 1 to 128, as said below
Outputs:
- image_grad: bfloat16 [196608, 1152], P('dp')
- text_grad: bfloat16 [196608, 1152], P('dp')
The draws below stay inside these ranges and needn't reach their ends.
Inputs may be any that keep to these rules, and one draw needn't show every extreme that they name: `round_masks`: each entry is a power of two below 256, the 2 entries are distinct, and one of them is 128; the same for all blocks.
All inputs are finite; a program needn't handle non-finite values.
Results may differ from the reference program's by a relative error of at most 0.0054.
Values may be sent and summed in bfloat16 or wider, within the bound.
No kernel may reach another device: no remote copies, remote signals or barrier semaphores. Data moves between devices by JAX's collectives and lax.ppermute only.
A program may use at most 128 MiB of HBM per device.

```python
import math
import jax
import jax.numpy as jnp
from jax import lax

D = 1152
TOK_DEV = 768
ROUNDS = 2
BATCH = 196608
N_DP = 256


def draw_round_masks(key, part):
    key = jax.random.fold_in(key, 7)
    nbits = int(math.log2(N_DP))
    lower_key = jax.random.fold_in(key, 1)
    order_key = jax.random.fold_in(key, 2)
    lower = jax.random.permutation(lower_key, jnp.arange(nbits - 1, dtype=jnp.int32))[:ROUNDS - 1]
    chosen = jnp.concatenate([lower, jnp.full((1,), nbits - 1, jnp.int32)])
    chosen = jax.random.permutation(order_key, chosen)
    return jnp.left_shift(jnp.ones((ROUNDS,), jnp.int32), chosen).astype(jnp.int32)


def shard_levels(stream_key, dims, shards, low, largest):
    def one(position, shards_of):
        steps = jax.random.uniform(jax.random.fold_in(jax.random.fold_in(stream_key, 6), position), (shards_of,), jnp.float32, low / len(shards), largest / len(shards))
        return jnp.repeat(jnp.exp(steps), dims[position] // shards_of).reshape((-1,) + (1,) * (len(dims) - position - 1))

    factor_of = one(*shards[0])
    for cut in shards[1:]:
        factor_of = factor_of * one(*cut)
    return factor_of


def scatter_about(stream_key, shape, scale, bound, pieces=(), kind=jnp.bfloat16):
    result = scale * jax.random.normal(stream_key, shape, jnp.float32)
    if pieces:
        result = result * shard_levels(stream_key, shape, pieces, -0.22, 0.18)
    return jnp.clip(result, -bound, bound).astype(kind)


def setup_inputs(seed: int = 0) -> dict:
    arg_keys = jax.random.split(jax.random.key(seed), 4)
    image_emb = scatter_about(arg_keys[0], (BATCH, D), 0.03, 0.19921875, ((0, 256),))
    text_emb = scatter_about(arg_keys[1], (BATCH, D), 0.03, 0.19921875, ((0, 256),))
    round_masks = draw_round_masks(jax.random.fold_in(arg_keys[3], 71), 0)
    return {"image_emb": image_emb, "text_emb": text_emb, "round_masks": round_masks}


def tile_coef(left, right, diag):
    logits = 10.0 * jnp.dot(left, right.T, preferred_element_type=jnp.float32) - 2.0
    return (jax.nn.sigmoid(logits) - diag).astype(jnp.bfloat16)


def reference(image_emb, text_emb, round_masks):
    images = image_emb.reshape(N_DP, TOK_DEV, D)
    texts = text_emb.reshape(N_DP, TOK_DEV, D)
    identity = jnp.eye(TOK_DEV, dtype=jnp.float32)

    def per_block(block):
        own_img = images[block]
        own_txt = texts[block]
        coef = tile_coef(own_img, own_txt, identity)
        img_total = 10.0 * jnp.dot(coef, own_txt, preferred_element_type=jnp.float32)
        txt_total = 10.0 * jnp.dot(coef.T, own_img, preferred_element_type=jnp.float32)
        for step in range(ROUNDS):
            other = jnp.bitwise_xor(block, round_masks[step]).astype(jnp.int32)
            far_img = images[other]
            far_txt = texts[other]
            first = tile_coef(own_img, far_txt, 0.0)
            img_total = img_total + 10.0 * jnp.dot(first, far_txt, preferred_element_type=jnp.float32)
            second = tile_coef(far_img, own_txt, 0.0)
            part = (10.0 * jnp.dot(second.T, far_img, preferred_element_type=jnp.float32)).astype(jnp.bfloat16)
            part = lax.optimization_barrier(part)
            txt_total = txt_total + part.astype(jnp.float32)
        return img_total.astype(jnp.bfloat16), txt_total.astype(jnp.bfloat16)

    img_grad, txt_grad = lax.map(per_block, jnp.arange(N_DP, dtype=jnp.int32))
    return img_grad.reshape(BATCH, D), txt_grad.reshape(BATCH, D)
```

```python
from functools import partial

import jax
import jax.numpy as jnp
from jax import lax
from jax.sharding import PartitionSpec as P

CHUNKS = 2


def swapped(block, bit):
    count = lax.axis_size("dp")
    return lax.ppermute(block, "dp", [(i, i ^ (1 << bit)) for i in range(count)])


def after(value, *earlier):
    return lax.optimization_barrier((value, *earlier))[0]


def tile_coef(left, right, diag):
    logits = 10.0 * jnp.dot(left, right.T, preferred_element_type=jnp.float32) - 2.0
    return (jax.nn.sigmoid(logits) - diag).astype(jnp.bfloat16)


def left_product(coef, right):
    return 10.0 * jnp.dot(coef, right, preferred_element_type=jnp.float32)


def transposed_product(coef, left):
    return 10.0 * lax.dot_general(
        coef, left, (((0,), (0,)), ((), ())), preferred_element_type=jnp.float32
    )


def chunks_of(array):
    rows = array.shape[0] // CHUNKS
    return [array[i * rows : (i + 1) * rows] for i in range(CHUNKS)]


def both_rounds(bit, top, image_emb, text_emb):
    rows = image_emb.shape[0]
    far_top = [swapped(piece, top) for piece in chunks_of(text_emb)]
    far_low = swapped(text_emb, bit)

    identity = (
        lax.broadcasted_iota(jnp.int32, (rows, rows), 0)
        == lax.broadcasted_iota(jnp.int32, (rows, rows), 1)
    ).astype(jnp.float32)
    coef = tile_coef(image_emb, text_emb, identity)
    img_total = left_product(coef, text_emb)
    txt_total = transposed_product(coef, image_emb)

    coef = tile_coef(image_emb, far_low, 0.0)
    part = transposed_product(coef, image_emb).astype(jnp.bfloat16)
    low_back = swapped(part, bit)
    img_total = img_total + left_product(coef, far_low)

    top_back = []
    for piece in far_top:
        coef = tile_coef(image_emb, piece, 0.0)
        part = transposed_product(coef, image_emb).astype(jnp.bfloat16)
        top_back.append(swapped(part, top))
        img_total = img_total + left_product(coef, piece)

    txt_total = txt_total + low_back.astype(jnp.float32)
    txt_grad = jnp.concatenate(
        [
            (total + back.astype(jnp.float32)).astype(jnp.bfloat16)
            for total, back in zip(chunks_of(txt_total), top_back)
        ]
    )
    return img_total.astype(jnp.bfloat16), txt_grad


def body(image_emb, text_emb, round_masks):
    top = lax.axis_size("dp").bit_length() - 2
    low = round_masks[0] + round_masks[1] - (1 << top)
    which = 31 - lax.clz(low)
    branches = [partial(both_rounds, bit, top) for bit in range(top)]
    return lax.switch(which, branches, image_emb, text_emb)


def solution(mesh):
    in_specs = (P("dp", None), P("dp", None), P())
    out_specs = (P("dp", None), P("dp", None))
    return jax.shard_map(body, mesh=mesh, in_specs=in_specs, out_specs=out_specs, check_vma=False)
```

```python
from functools import partial

import jax
import jax.numpy as jnp
from jax import lax
from jax.experimental import pallas as pl
from jax.experimental.pallas import tpu as pltpu
from jax.sharding import PartitionSpec as P

SIDE = 256
PIECES = 3
RELAY_PIECES = 4


def swapped(block, mask):
    count = lax.axis_size("dp")
    return lax.ppermute(block, "dp", [(i, i ^ mask) for i in range(count)])


def after(value, earlier):
    return lax.optimization_barrier((value, earlier))[0]


def split(array, count):
    rows = array.shape[0] // count
    return [array[i * rows : (i + 1) * rows] for i in range(count)]


def split_in_turn(array, count):
    rows = array.shape[0] // count
    pieces = []
    for i in range(count):
        pieces.append(array[i * rows : (i + 1) * rows])
        array = after(array, pieces[-1])
    return pieces


def joined(total, pieces):
    result = total.astype(jnp.bfloat16)
    start = 0
    for piece in pieces:
        rows = piece.shape[0]
        added = total[start : start + rows] + piece.astype(jnp.float32)
        result = lax.dynamic_update_slice(result, added.astype(jnp.bfloat16), (start, 0))
        start += rows
    return result


def step_of(rows):
    return SIDE if rows % SIDE == 0 else rows


def tile_sum_kernel(counts, diagonal, has_extra, mine_ref, *refs):
    others, refs = refs[: len(counts)], refs[len(counts) :]
    extra_ref = refs[0] if has_extra else None
    out_ref, total = refs[-3], refs[-2]
    held = refs[-1]
    start = 0
    for ref, rows in zip(others, counts):
        held[start : start + rows, :] = ref[...]
        start += rows
    rows = mine_ref.shape[0]
    step = step_of(rows)

    @pl.loop(0, rows // step)
    def _(i):
        here = pl.ds(pl.multiple_of(i * step, step), step)
        total[...] = jnp.zeros_like(total)

        @pl.loop(0, start // SIDE)
        def _(k):
            there = pl.ds(pl.multiple_of(k * SIDE, SIDE), SIDE)
            far = held[there, :]
            logits = 10.0 * lax.dot_general(
                mine_ref[here, :],
                far,
                (((1,), (1,)), ((), ())),
                preferred_element_type=jnp.float32,
            ) - 2.0
            coef = 1.0 / (1.0 + jnp.exp(-logits))
            if diagonal:
                row = lax.broadcasted_iota(jnp.int32, coef.shape, 0) + i * step
                col = lax.broadcasted_iota(jnp.int32, coef.shape, 1) + k * SIDE
                coef = coef - (row == col).astype(jnp.float32)
            total[...] += jnp.dot(
                coef.astype(jnp.bfloat16), far, preferred_element_type=jnp.float32
            )

        result = 10.0 * total[...]
        if has_extra:
            result = result + extra_ref[here, :].astype(jnp.float32)
        out_ref[here, :] = result.astype(out_ref.dtype)


def tile_sum(mine, others, diagonal=False, extra=None, dtype=jnp.bfloat16):
    rows, width = mine.shape
    counts = [other.shape[0] for other in others]
    across = sum(counts)
    operands = [mine, *others] + ([] if extra is None else [extra])
    return pl.pallas_call(
        partial(tile_sum_kernel, counts, diagonal, extra is not None),
        out_shape=jax.ShapeDtypeStruct((rows, width), dtype),
        in_specs=[pl.BlockSpec(memory_space=pltpu.VMEM)] * len(operands),
        out_specs=pl.BlockSpec(memory_space=pltpu.VMEM),
        scratch_shapes=[
            pltpu.VMEM((step_of(rows), width), jnp.float32),
            pltpu.VMEM((across, width), jnp.bfloat16),
        ],
        compiler_params=pltpu.CompilerParams(vmem_limit_bytes=24 * 1024 * 1024),
        cost_estimate=pl.CostEstimate(
            flops=4 * rows * across * width,
            bytes_accessed=2 * width * (2 * rows + across),
            transcendentals=rows * across,
        ),
    )(*operands)


def straight(which, lows, top, image_emb, text_emb):
    def swapped_low(block):
        return lax.switch(which, [partial(swapped, mask=low) for low in lows], block)

    far_top = [swapped(piece, top) for piece in split_in_turn(text_emb, PIECES)]
    far_low = swapped_low(text_emb)
    own = tile_sum(text_emb, [image_emb], diagonal=True, dtype=jnp.float32)
    low_part = tile_sum(far_low, [image_emb])
    top_parts = [tile_sum(piece, [image_emb]) for piece in far_top]
    top_back = [swapped(part, top) for part in top_parts]
    low_back = swapped_low(after(low_part, top_parts))
    image_grad = tile_sum(image_emb, [text_emb, far_low, *far_top], diagonal=True)
    return image_grad, joined(own + low_back.astype(jnp.float32), top_back)


def relayed(low, top, image_emb, text_emb):
    pieces = split(text_emb, RELAY_PIECES)
    far_low = [swapped(piece, low) for piece in pieces]
    far_top = [swapped(piece, low ^ top) for piece in far_low]
    own = tile_sum(text_emb, [image_emb], diagonal=True, dtype=jnp.float32)
    last = own
    back = []
    for low_piece, top_piece in zip(far_low, far_top):
        low_part = tile_sum(after(low_piece, last), [image_emb], dtype=jnp.float32)
        last = tile_sum(after(top_piece, low_part), [image_emb])
        both = low_part + swapped(last, low ^ top).astype(jnp.float32)
        back.append(swapped(both.astype(jnp.bfloat16), low))
    image_grad = tile_sum(
        after(image_emb, last), [text_emb, *far_low, *far_top], diagonal=True
    )
    return image_grad, joined(own, back)


def body(image_emb, text_emb, round_masks):
    top = lax.axis_size("dp") // 2
    which = 31 - lax.clz(round_masks[0] + round_masks[1] - top)
    lows = [1 << bit for bit in range(top.bit_length() - 1)]
    across, along = lows[:-2], lows[-2:]
    plans = [partial(straight, which, across, top)]
    plans += [partial(relayed, low, top) for low in along]
    return lax.switch(which - (len(across) - 1), plans, image_emb, text_emb)


def solution(mesh):
    in_specs = (P("dp", None), P("dp", None), P())
    out_specs = (P("dp", None), P("dp", None))
    return jax.shard_map(body, mesh=mesh, in_specs=in_specs, out_specs=out_specs, check_vma=False)
```

```python
import math
from functools import partial

import jax
import jax.numpy as jnp
from jax import lax
from jax.experimental import pallas as pl
from jax.experimental.pallas import tpu as pltpu
from jax.sharding import PartitionSpec as P

SIDE = 256
COLUMNS = 384
BACK = (1, 2)
RELAY = (1, 1, 1, 1)


def swapped(block, mask):
    count = lax.axis_size("dp")
    return lax.ppermute(block, "dp", [(i, i ^ mask) for i in range(count)])


def after(value, earlier):
    return lax.optimization_barrier((value, earlier))[0]


def spans(rows, parts):
    ends = [rows * sum(parts[:i]) // sum(parts) for i in range(len(parts) + 1)]
    return list(zip(ends[:-1], ends[1:]))


def tile_sum_kernel(counts, diagonal, mine_rows, mine_ref, *refs):
    others, refs = refs[: len(counts)], refs[len(counts) :]
    out_ref, coefs = refs[:2]
    if len(others) == 1:
        held = others[0]
    else:
        held = refs[2]
        start = 0
        for ref, rows in zip(others, counts):
            held[start : start + rows, :] = ref[...]
            start += rows
    across, width = held.shape

    @pl.loop(0, across // SIDE)
    def _(k):
        there = pl.ds(pl.multiple_of(k * SIDE, SIDE), SIDE)
        logits = 10.0 * lax.dot_general(
            mine_ref[slice(*mine_rows), :],
            held[there, :],
            (((1,), (1,)), ((), ())),
            preferred_element_type=jnp.float32,
        ) - 2.0
        coef = 1.0 / (1.0 + jnp.exp(-logits))
        if diagonal:
            row = lax.broadcasted_iota(jnp.int32, coef.shape, 0)
            col = lax.broadcasted_iota(jnp.int32, coef.shape, 1) + k * SIDE
            coef = coef - (row == col).astype(jnp.float32)
        coefs[:, there] = coef.astype(jnp.bfloat16)

    @pl.loop(0, width // COLUMNS)
    def _(n):
        columns = pl.ds(pl.multiple_of(n * COLUMNS, COLUMNS), COLUMNS)
        out_ref[:, columns] = (
            10.0 * jnp.dot(coefs[...], held[:, columns], preferred_element_type=jnp.float32)
        ).astype(out_ref.dtype)


def tile_sum(mine, others, diagonal=False, dtype=jnp.bfloat16, mine_rows=None):
    width = mine.shape[1]
    mine_rows = mine_rows or (0, mine.shape[0])
    rows = mine_rows[1] - mine_rows[0]
    counts = [other.shape[0] for other in others]
    across = sum(counts)
    scratch = [pltpu.VMEM((rows, across), jnp.bfloat16)]
    if len(others) > 1:
        scratch.append(pltpu.VMEM((across, width), jnp.bfloat16))
    return pl.pallas_call(
        partial(tile_sum_kernel, counts, diagonal, mine_rows),
        out_shape=jax.ShapeDtypeStruct((rows, width), dtype),
        in_specs=[pl.BlockSpec(memory_space=pltpu.VMEM)] * (1 + len(others)),
        out_specs=pl.BlockSpec(memory_space=pltpu.VMEM),
        scratch_shapes=scratch,
        compiler_params=pltpu.CompilerParams(vmem_limit_bytes=28 * 1024 * 1024),
        cost_estimate=pl.CostEstimate(
            flops=4 * rows * across * width,
            bytes_accessed=2 * width * (2 * rows + across),
            transcendentals=rows * across,
        ),
    )(mine, *others)


def add_rows_kernel(total_ref, piece_ref, *refs):
    out_ref = refs[-1]
    out_ref[...] = (total_ref[...] + piece_ref[...].astype(jnp.float32)).astype(out_ref.dtype)


def joined(total, pieces):
    result, start = None, 0
    for piece in pieces:
        rows, width = piece.shape
        step = math.gcd(start, rows)
        here = pl.BlockSpec((step, width), lambda i, first=start // step: (first + i, 0))
        operands, alias = [total, piece], {}
        specs = [here, pl.BlockSpec((step, width), lambda i: (i, 0))]
        if result is not None:
            operands.append(result)
            specs.append(pl.BlockSpec(memory_space=pl.ANY))
            alias = {2: 0}
        result = pl.pallas_call(
            add_rows_kernel,
            grid=(rows // step,),
            out_shape=jax.ShapeDtypeStruct(total.shape, piece.dtype),
            in_specs=specs,
            out_specs=here,
            input_output_aliases=alias,
        )(*operands)
        start += rows
    return result


def straight(which, lows, top, image_emb, text_emb):
    def swapped_low(block):
        return lax.switch(which, [partial(swapped, mask=low) for low in lows], block)

    far_top = swapped(text_emb, top)
    far_low = swapped_low(text_emb)
    own = tile_sum(text_emb, [image_emb], diagonal=True, dtype=jnp.float32)
    low_part = tile_sum(far_low, [image_emb])
    top_parts, last = [], low_part
    for span in spans(far_top.shape[0], BACK):
        last = tile_sum(after(far_top, last), [image_emb], mine_rows=span)
        top_parts.append(last)
    top_back = [swapped(part, top) for part in top_parts]
    low_back = swapped_low(after(low_part, top_parts))
    image_grad = tile_sum(image_emb, [text_emb, far_low, far_top], diagonal=True)
    return image_grad, joined(own + low_back.astype(jnp.float32), top_back)


def relayed(low, top, image_emb, text_emb):
    far_low, far_top, back = [], [], []
    for start, end in spans(text_emb.shape[0], RELAY):
        piece = text_emb[start:end]
        if far_low:
            piece = after(piece, far_low[-1])
        far_low.append(swapped(piece, low))
        far_top.append(swapped(far_low[-1], low ^ top))
    own = tile_sum(text_emb, [image_emb], diagonal=True, dtype=jnp.float32)
    for low_piece, top_piece in zip(far_low, far_top):
        low_part = tile_sum(low_piece, [image_emb], dtype=jnp.float32)
        top_part = tile_sum(top_piece, [image_emb])
        both = low_part + swapped(top_part, low ^ top).astype(jnp.float32)
        back.append(swapped(both.astype(jnp.bfloat16), low))
    image_grad = tile_sum(image_emb, [text_emb, *far_low, *far_top], diagonal=True)
    return image_grad, joined(own, back)


def body(image_emb, text_emb, round_masks):
    top = lax.axis_size("dp") // 2
    which = 31 - lax.clz(round_masks[0] + round_masks[1] - top)
    lows = [1 << bit for bit in range(top.bit_length() - 1)]
    across, along = lows[:-2], lows[-2:]
    plans = [partial(straight, which, across, top)]
    plans += [partial(relayed, low, top) for low in along]
    return lax.switch(which - (len(across) - 1), plans, image_emb, text_emb)


def solution(mesh):
    in_specs = (P("dp", None), P("dp", None), P())
    out_specs = (P("dp", None), P("dp", None))
    return jax.shard_map(body, mesh=mesh, in_specs=in_specs, out_specs=out_specs, check_vma=False)
```

```python
from functools import partial

import jax
import jax.numpy as jnp
from jax import lax
from jax.experimental import pallas as pl
from jax.experimental.pallas import tpu as pltpu
from jax.sharding import PartitionSpec as P

SIDE = 256
COLUMNS = 384
BACK = (1, 5)
RELAY = (1, 1, 1)


def swapped(block, mask):
    count = lax.axis_size("dp")
    return lax.ppermute(block, "dp", [(i, i ^ mask) for i in range(count)])


def after(value, earlier):
    return lax.optimization_barrier((value, earlier))[0]


def spans(rows, parts):
    ends = [rows * sum(parts[:i]) // sum(parts) for i in range(len(parts) + 1)]
    return list(zip(ends[:-1], ends[1:]))


def tile_sum_kernel(counts, diagonal, has_extra, side, columns, mine_ref, *refs):
    others, refs = refs[: len(counts)], refs[len(counts) :]
    if has_extra:
        extra_ref, refs = refs[0], refs[1:]
    out_ref, coefs = refs[:2]
    if len(others) == 1:
        held = others[0]
    else:
        held = refs[2]
        start = 0
        for ref, rows in zip(others, counts):
            held[start : start + rows, :] = ref[...]
            start += rows
    across, width = held.shape

    @pl.loop(0, across // side)
    def _(k):
        there = pl.ds(pl.multiple_of(k * side, side), side)
        logits = 10.0 * lax.dot_general(
            mine_ref[...],
            held[there, :],
            (((1,), (1,)), ((), ())),
            preferred_element_type=jnp.float32,
        ) - 2.0
        coef = 1.0 / (1.0 + jnp.exp(-logits))
        if diagonal:
            row = lax.broadcasted_iota(jnp.int32, coef.shape, 0)
            col = lax.broadcasted_iota(jnp.int32, coef.shape, 1) + k * side
            coef = coef - (row == col).astype(jnp.float32)
        coefs[:, there] = coef.astype(jnp.bfloat16)

    @pl.loop(0, width // columns)
    def _(n):
        here = pl.ds(pl.multiple_of(n * columns, columns), columns)
        result = 10.0 * jnp.dot(
            coefs[...], held[:, here], preferred_element_type=jnp.float32
        )
        if has_extra:
            result = result + extra_ref[:, here]
        out_ref[:, here] = result.astype(out_ref.dtype)


def tile_sum(
    mine,
    others,
    diagonal=False,
    dtype=jnp.bfloat16,
    span=None,
    extra=None,
    blocks=(SIDE, COLUMNS),
    weight=8,
):
    width = mine.shape[1]
    first, end = span or (0, mine.shape[0])
    rows = end - first
    counts = [other.shape[0] for other in others]
    across = sum(counts)
    operands = [mine, *others] + ([] if extra is None else [extra])
    whole = pl.BlockSpec(memory_space=pltpu.VMEM)
    some = pl.BlockSpec((pl.Element(rows), pl.Element(width)), lambda _: (first, 0))
    scratch = [pltpu.VMEM((rows, across), jnp.bfloat16)]
    if len(others) > 1:
        scratch.append(pltpu.VMEM((across, width), jnp.bfloat16))
    return pl.pallas_call(
        partial(tile_sum_kernel, counts, diagonal, extra is not None, *blocks),
        grid=() if span is None else (1,),
        out_shape=jax.ShapeDtypeStruct((rows, width), dtype),
        in_specs=[whole if span is None else some] + [whole] * (len(operands) - 1),
        out_specs=whole,
        scratch_shapes=scratch,
        compiler_params=pltpu.CompilerParams(vmem_limit_bytes=28 * 1024 * 1024),
        cost_estimate=pl.CostEstimate(
            flops=weight * 4 * rows * across * width,
            bytes_accessed=weight * 2 * width * (2 * rows + across),
            transcendentals=weight * rows * across,
        ),
    )(*operands)


def add_rows_kernel(total_ref, piece_ref, *refs):
    out_ref = refs[-1]
    out_ref[...] = (total_ref[...] + piece_ref[...].astype(jnp.float32)).astype(out_ref.dtype)


def joined(total, pieces):
    result, start = None, 0
    for piece in pieces:
        rows, width = piece.shape
        here = pl.BlockSpec(
            (pl.Element(rows), pl.Element(width)), lambda i, first=start: (first, 0)
        )
        operands, alias = [total, piece], {}
        specs = [here, pl.BlockSpec((rows, width), lambda i: (0, 0))]
        if result is not None:
            operands.append(result)
            specs.append(pl.BlockSpec(memory_space=pl.ANY))
            alias = {2: 0}
        result = pl.pallas_call(
            add_rows_kernel,
            grid=(1,),
            out_shape=pltpu.HBM(total.shape, piece.dtype),
            in_specs=specs,
            out_specs=here,
            input_output_aliases=alias,
            compiler_params=pltpu.CompilerParams(vmem_limit_bytes=28 * 1024 * 1024),
        )(*operands)
        start += rows
    return result


def straight(which, lows, top, image_emb, text_emb):
    def swapped_low(block):
        return lax.switch(which, [partial(swapped, mask=low) for low in lows], block)

    far_top = swapped(text_emb, top)
    far_low = swapped_low(text_emb)
    own = tile_sum(text_emb, [image_emb], diagonal=True, dtype=jnp.float32)
    low_part = tile_sum(far_low, [image_emb])
    image_total = tile_sum(
        after(image_emb, (own, low_part)), [text_emb, far_low], diagonal=True, dtype=jnp.float32
    )
    top_parts, last = [], image_total
    for span in spans(far_top.shape[0], BACK):
        blocks = (SIDE, COLUMNS) if top_parts else image_emb.shape
        last = tile_sum(after(far_top, last), [image_emb], span=span, blocks=blocks)
        top_parts.append(last)
    top_back = [swapped(part, top) for part in top_parts]
    low_back = swapped_low(after(low_part, top_parts))
    image_grad = tile_sum(image_emb, [far_top], extra=image_total)
    return image_grad, joined(own + low_back.astype(jnp.float32), top_back)


def relayed(low, top, image_emb, text_emb):
    summed = partial(tile_sum, weight=1)
    far_low, far_top, back = [], [], []
    for first, end in spans(text_emb.shape[0], RELAY):
        piece = text_emb[first:end]
        if far_low:
            piece = after(piece, far_low[-1])
        far_low.append(swapped(piece, low))
        far_top.append(swapped(far_low[-1], low ^ top))
    own = summed(text_emb, [image_emb], diagonal=True, dtype=jnp.float32)
    image_total = summed(
        image_emb, [text_emb, *far_low], diagonal=True, dtype=jnp.float32
    )
    far_top[-1] = after(far_top[-1], image_total)
    for low_piece, top_piece in zip(far_low, far_top):
        low_part = summed(low_piece, [image_emb], dtype=jnp.float32)
        top_part = summed(top_piece, [image_emb])
        both = low_part + swapped(top_part, low ^ top).astype(jnp.float32)
        back.append(swapped(both.astype(jnp.bfloat16), low))
    image_grad = summed(image_emb, far_top, extra=image_total)
    return image_grad, joined(own, back)


def body(image_emb, text_emb, round_masks):
    top = lax.axis_size("dp") // 2
    which = 31 - lax.clz(round_masks[0] + round_masks[1] - top)
    lows = [1 << bit for bit in range(top.bit_length() - 1)]
    across, along = lows[:-2], lows[-2:]
    plans = [partial(straight, which, across, top)]
    plans += [partial(relayed, low, top) for low in along]
    return lax.switch(which - (len(across) - 1), plans, image_emb, text_emb)


def solution(mesh):
    in_specs = (P("dp", None), P("dp", None), P())
    out_specs = (P("dp", None), P("dp", None))
    return jax.shard_map(body, mesh=mesh, in_specs=in_specs, out_specs=out_specs, check_vma=False)
```

```python
from functools import partial

import jax
import jax.numpy as jnp
from jax import lax
from jax.experimental import pallas as pl
from jax.experimental.pallas import tpu as pltpu
from jax.sharding import PartitionSpec as P

SIDE = 256
COLUMNS = 384
ROWS = 640
BACK = (1, 5)
RELAY = ((1,) * 2, (1,) * 4)


def swapped(block, mask):
    count = lax.axis_size("dp")
    return lax.ppermute(block, "dp", [(i, i ^ mask) for i in range(count)])


def after(value, earlier):
    return lax.optimization_barrier((value, earlier))[0]


def spans(rows, parts):
    ends = [rows * sum(parts[:i]) // sum(parts) for i in range(len(parts) + 1)]
    return list(zip(ends[:-1], ends[1:]))


def tile_sum_kernel(counts, diagonal, has_extra, side, columns, mine_ref, *refs):
    others, refs = refs[: len(counts)], refs[len(counts) :]
    if has_extra:
        extra_ref, refs = refs[0], refs[1:]
    out_ref, coefs = refs[:2]
    if len(others) == 1:
        held = others[0]
    else:
        held = refs[2]
        start = 0
        for ref, rows in zip(others, counts):
            held[start : start + rows, :] = ref[...]
            start += rows
    across, width = held.shape
    rows = coefs.shape[0]

    @pl.loop(0, mine_ref.shape[0] // rows)
    def _(i):
        mine = pl.ds(pl.multiple_of(i * rows, rows), rows)

        @pl.loop(0, across // side)
        def _(k):
            there = pl.ds(pl.multiple_of(k * side, side), side)
            logits = 10.0 * lax.dot_general(
                mine_ref[mine, :],
                held[there, :],
                (((1,), (1,)), ((), ())),
                preferred_element_type=jnp.float32,
            ) - 2.0
            coef = 1.0 / (1.0 + jnp.exp(-logits))
            if diagonal:
                row = lax.broadcasted_iota(jnp.int32, coef.shape, 0) + i * rows
                col = lax.broadcasted_iota(jnp.int32, coef.shape, 1) + k * side
                coef = coef - (row == col).astype(jnp.float32)
            coefs[:, there] = coef.astype(jnp.bfloat16)

        @pl.loop(0, width // columns)
        def _(n):
            here = pl.ds(pl.multiple_of(n * columns, columns), columns)
            result = 10.0 * jnp.dot(
                coefs[...], held[:, here], preferred_element_type=jnp.float32
            )
            if has_extra:
                result = result + extra_ref[mine, here]
            out_ref[mine, here] = result.astype(out_ref.dtype)


def tile_sum(
    mine,
    others,
    diagonal=False,
    dtype=jnp.bfloat16,
    span=None,
    extra=None,
    blocks=(SIDE, COLUMNS),
    weight=8,
):
    width = mine.shape[1]
    first, end = span or (0, mine.shape[0])
    rows = end - first
    counts = [other.shape[0] for other in others]
    across = sum(counts)
    operands = [mine, *others] + ([] if extra is None else [extra])
    whole = pl.BlockSpec(memory_space=pltpu.VMEM)
    some = pl.BlockSpec((pl.Element(rows), pl.Element(width)), lambda _: (first, 0))
    step = rows // 2 if rows > ROWS else rows
    scratch = [pltpu.VMEM((step, across), jnp.bfloat16)]
    if len(others) > 1:
        scratch.append(pltpu.VMEM((across, width), jnp.bfloat16))
    return pl.pallas_call(
        partial(tile_sum_kernel, counts, diagonal, extra is not None, *blocks),
        grid=() if span is None else (1,),
        out_shape=jax.ShapeDtypeStruct((rows, width), dtype),
        in_specs=[whole if span is None else some] + [whole] * (len(operands) - 1),
        out_specs=whole,
        scratch_shapes=scratch,
        compiler_params=pltpu.CompilerParams(vmem_limit_bytes=28 * 1024 * 1024),
        cost_estimate=pl.CostEstimate(
            flops=weight * 4 * rows * across * width,
            bytes_accessed=weight * 2 * width * (2 * rows + across),
            transcendentals=weight * rows * across,
        ),
    )(*operands)


def add_rows_kernel(total_ref, piece_ref, *refs):
    out_ref = refs[-1]
    out_ref[...] = (total_ref[...] + piece_ref[...].astype(jnp.float32)).astype(out_ref.dtype)


def joined(total, pieces):
    result, start = None, 0
    for piece in pieces:
        rows, width = piece.shape
        here = pl.BlockSpec(
            (pl.Element(rows), pl.Element(width)), lambda i, first=start: (first, 0)
        )
        operands, alias = [total, piece], {}
        specs = [here, pl.BlockSpec((rows, width), lambda i: (0, 0))]
        if result is not None:
            operands.append(result)
            specs.append(pl.BlockSpec(memory_space=pl.ANY))
            alias = {2: 0}
        result = pl.pallas_call(
            add_rows_kernel,
            grid=(1,),
            out_shape=pltpu.HBM(total.shape, piece.dtype),
            in_specs=specs,
            out_specs=here,
            input_output_aliases=alias,
            compiler_params=pltpu.CompilerParams(vmem_limit_bytes=28 * 1024 * 1024),
        )(*operands)
        start += rows
    return result


def straight(which, lows, top, image_emb, text_emb):
    def swapped_low(block):
        return lax.switch(which, [partial(swapped, mask=low) for low in lows], block)

    far_top = swapped(text_emb, top)
    far_low = swapped_low(text_emb)
    own = tile_sum(text_emb, [image_emb], diagonal=True, dtype=jnp.float32)
    low_part = tile_sum(far_low, [image_emb])
    image_total = tile_sum(
        after(image_emb, (own, low_part)), [text_emb, far_low], diagonal=True, dtype=jnp.float32
    )
    top_parts, last = [], image_total
    for span in spans(far_top.shape[0], BACK):
        blocks = (SIDE, COLUMNS) if top_parts else image_emb.shape
        last = tile_sum(after(far_top, last), [image_emb], span=span, blocks=blocks)
        top_parts.append(last)
    top_back = [swapped(part, top) for part in top_parts]
    low_back = swapped_low(after(low_part, top_parts))
    image_grad = tile_sum(image_emb, [far_top], extra=image_total)
    return image_grad, joined(own + low_back.astype(jnp.float32), top_back)


def relayed(low, top, shares, image_emb, text_emb):
    summed = partial(tile_sum, weight=1)
    far_low, far_top, back = [], [], []
    for first, end in spans(text_emb.shape[0], shares):
        piece = text_emb[first:end]
        if far_low:
            piece = after(piece, far_low[-1])
        far_low.append(swapped(piece, low))
        far_top.append(swapped(far_low[-1], low ^ top))
    own = summed(text_emb, [image_emb], diagonal=True, dtype=jnp.float32)
    image_total = summed(
        image_emb, [text_emb, *far_low], diagonal=True, dtype=jnp.float32
    )
    far_top[-1] = after(far_top[-1], image_total)
    for low_piece, top_piece in zip(far_low, far_top):
        low_part = summed(low_piece, [image_emb], dtype=jnp.float32)
        top_part = summed(top_piece, [image_emb])
        both = low_part + swapped(top_part, low ^ top).astype(jnp.float32)
        back.append(swapped(both.astype(jnp.bfloat16), low))
    image_grad = summed(image_emb, far_top, extra=image_total)
    return image_grad, joined(own, back)


def body(image_emb, text_emb, round_masks):
    top = lax.axis_size("dp") // 2
    which = 31 - lax.clz(round_masks[0] + round_masks[1] - top)
    lows = [1 << bit for bit in range(top.bit_length() - 1)]
    across, along = lows[:-2], lows[-2:]
    plans = [partial(straight, which, across, top)]
    plans += [partial(relayed, low, top, shares) for low, shares in zip(along, RELAY)]
    return lax.switch(which - (len(across) - 1), plans, image_emb, text_emb)


def solution(mesh):
    in_specs = (P("dp", None), P("dp", None), P())
    out_specs = (P("dp", None), P("dp", None))
    return jax.shard_map(body, mesh=mesh, in_specs=in_specs, out_specs=out_specs, check_vma=False)
```

```python
from functools import partial

import jax
import jax.numpy as jnp
from jax import lax
from jax.experimental import pallas as pl
from jax.experimental.pallas import tpu as pltpu
from jax.sharding import PartitionSpec as P

SIDE = 256
COLUMNS = 384
ROWS = 640
BACK = (1, 5)
RELAY = ((1,) * 2, (1,) * 4)


def swapped(block, mask):
    count = lax.axis_size("dp")
    return lax.ppermute(block, "dp", [(i, i ^ mask) for i in range(count)])


def after(value, earlier):
    return lax.optimization_barrier((value, earlier))[0]


def spans(rows, parts):
    ends = [rows * sum(parts[:i]) // sum(parts) for i in range(len(parts) + 1)]
    return list(zip(ends[:-1], ends[1:]))


def tile_sum_kernel(counts, diagonal, has_extra, side, columns, mine_ref, *refs):
    others, refs = refs[: len(counts)], refs[len(counts) :]
    if has_extra:
        extra_ref, refs = refs[0], refs[1:]
    out_ref, coefs = refs[:2]
    if len(others) == 1:
        held = others[0]
    else:
        held = refs[2]
        start = 0
        for ref, rows in zip(others, counts):
            held[start : start + rows, :] = ref[...]
            start += rows
    across, width = held.shape
    rows = coefs.shape[0]

    @pl.loop(0, mine_ref.shape[0] // rows)
    def _(i):
        mine = pl.ds(pl.multiple_of(i * rows, rows), rows)

        @pl.loop(0, across // side)
        def _(k):
            there = pl.ds(pl.multiple_of(k * side, side), side)
            logits = 10.0 * lax.dot_general(
                mine_ref[mine, :],
                held[there, :],
                (((1,), (1,)), ((), ())),
                preferred_element_type=jnp.float32,
            ) - 2.0
            coef = 1.0 / (1.0 + jnp.exp(-logits))
            if diagonal:
                row = lax.broadcasted_iota(jnp.int32, coef.shape, 0) + i * rows
                col = lax.broadcasted_iota(jnp.int32, coef.shape, 1) + k * side
                coef = coef - (row == col).astype(jnp.float32)
            coefs[:, there] = coef.astype(jnp.bfloat16)

        @pl.loop(0, width // columns)
        def _(n):
            here = pl.ds(pl.multiple_of(n * columns, columns), columns)
            result = 10.0 * jnp.dot(
                coefs[...], held[:, here], preferred_element_type=jnp.float32
            )
            if has_extra:
                result = result + extra_ref[mine, here]
            out_ref[mine, here] = result.astype(out_ref.dtype)


def tile_sum(
    mine,
    others,
    diagonal=False,
    dtype=jnp.bfloat16,
    span=None,
    extra=None,
    blocks=(SIDE, COLUMNS),
    weight=8,
):
    width = mine.shape[1]
    first, end = span or (0, mine.shape[0])
    rows = end - first
    counts = [other.shape[0] for other in others]
    across = sum(counts)
    operands = [mine, *others] + ([] if extra is None else [extra])
    whole = pl.BlockSpec(memory_space=pltpu.VMEM)
    some = pl.BlockSpec((pl.Element(rows), pl.Element(width)), lambda _: (first, 0))
    step = rows // 2 if rows > ROWS else rows
    scratch = [pltpu.VMEM((step, across), jnp.bfloat16)]
    if len(others) > 1:
        scratch.append(pltpu.VMEM((across, width), jnp.bfloat16))
    return pl.pallas_call(
        partial(tile_sum_kernel, counts, diagonal, extra is not None, *blocks),
        grid=() if span is None else (1,),
        out_shape=jax.ShapeDtypeStruct((rows, width), dtype),
        in_specs=[whole if span is None else some] + [whole] * (len(operands) - 1),
        out_specs=whole,
        scratch_shapes=scratch,
        compiler_params=pltpu.CompilerParams(vmem_limit_bytes=28 * 1024 * 1024),
        cost_estimate=pl.CostEstimate(
            flops=weight * 4 * rows * across * width,
            bytes_accessed=weight * 2 * width * (2 * rows + across),
            transcendentals=weight * rows * across,
        ),
    )(*operands)


def add_rows_kernel(total_ref, piece_ref, *refs):
    out_ref = refs[-1]
    out_ref[...] = (total_ref[...] + piece_ref[...].astype(jnp.float32)).astype(out_ref.dtype)


def joined(total, pieces):
    result, start = None, 0
    for piece in pieces:
        rows, width = piece.shape
        step = rows // 2 if rows > COLUMNS else rows
        here = pl.BlockSpec(
            (pl.Element(step), pl.Element(width)),
            lambda i, first=start, step=step: (pl.multiple_of(first + i * step, 16), 0),
        )
        operands, alias = [total, piece], {}
        specs = [here, pl.BlockSpec((step, width), lambda i: (i, 0))]
        if result is not None:
            operands.append(result)
            specs.append(pl.BlockSpec(memory_space=pl.ANY))
            alias = {2: 0}
        result = pl.pallas_call(
            add_rows_kernel,
            grid=(rows // step,),
            out_shape=pltpu.HBM(total.shape, piece.dtype),
            in_specs=specs,
            out_specs=here,
            input_output_aliases=alias,
            compiler_params=pltpu.CompilerParams(vmem_limit_bytes=28 * 1024 * 1024),
        )(*operands)
        start += rows
    return result


def straight(which, lows, top, image_emb, text_emb):
    def swapped_low(block):
        return lax.switch(which, [partial(swapped, mask=low) for low in lows], block)

    far_top = swapped(text_emb, top)
    far_low = swapped_low(text_emb)
    own = tile_sum(text_emb, [image_emb], diagonal=True, dtype=jnp.float32)
    low_part = tile_sum(far_low, [image_emb])
    image_total = tile_sum(
        after(image_emb, (own, low_part)), [text_emb, far_low], diagonal=True, dtype=jnp.float32
    )
    top_parts, last = [], image_total
    for span in spans(far_top.shape[0], BACK):
        blocks = (SIDE, COLUMNS) if top_parts else image_emb.shape
        last = tile_sum(after(far_top, last), [image_emb], span=span, blocks=blocks)
        top_parts.append(last)
    top_back = [swapped(part, top) for part in top_parts]
    low_back = swapped_low(after(low_part, top_parts))
    image_grad = tile_sum(image_emb, [far_top], extra=image_total)
    return image_grad, joined(own + low_back.astype(jnp.float32), top_back)


def relayed(low, top, shares, image_emb, text_emb):
    summed = partial(tile_sum, weight=1)
    far_low, far_top, back = [], [], []
    for first, end in spans(text_emb.shape[0], shares):
        piece = text_emb[first:end]
        if far_low:
            piece = after(piece, far_low[-1])
        far_low.append(swapped(piece, low))
        far_top.append(swapped(far_low[-1], low ^ top))
    own = summed(text_emb, [image_emb], diagonal=True, dtype=jnp.float32)
    image_total = summed(
        image_emb, [text_emb, *far_low], diagonal=True, dtype=jnp.float32
    )
    far_top[-1] = after(far_top[-1], image_total)
    for low_piece, top_piece in zip(far_low, far_top):
        low_part = summed(low_piece, [image_emb], dtype=jnp.float32)
        top_part = summed(top_piece, [image_emb])
        both = low_part + swapped(top_part, low ^ top).astype(jnp.float32)
        back.append(swapped(both.astype(jnp.bfloat16), low))
    image_grad = summed(image_emb, far_top, extra=image_total)
    return image_grad, joined(own, back)


def body(image_emb, text_emb, round_masks):
    top = lax.axis_size("dp") // 2
    which = 31 - lax.clz(round_masks[0] + round_masks[1] - top)
    lows = [1 << bit for bit in range(top.bit_length() - 1)]
    across, along = lows[:-2], lows[-2:]
    plans = [partial(straight, which, across, top)]
    plans += [partial(relayed, low, top, shares) for low, shares in zip(along, RELAY)]
    return lax.switch(which - (len(across) - 1), plans, image_emb, text_emb)


def solution(mesh):
    in_specs = (P("dp", None), P("dp", None), P())
    out_specs = (P("dp", None), P("dp", None))
    return jax.shard_map(body, mesh=mesh, in_specs=in_specs, out_specs=out_specs, check_vma=False)
```
